32 devices in a mesh: dp: 16 (over z, y, x), tensor: 2 (over core).
Axes of the slice: x: 2, y: 2, z: 4, core: 2. Of those that a mesh axis runs over, the one named last changes fastest.
Arguments:
- inputs: bfloat16 [16384, 1024], P('dp'), may hold values from -6 to 6
- segments: int32 [16, 1024], P('dp'), may hold values from 0 to 3, never falling along the last dimension, each value on 1 to 512 neighbouring positions
- mixer_gain: float32 [1024], replicated, may hold values from 0.5 to 1.5
- ssm_gate: bfloat16 [1024, 1536], P('dp', 'tensor'), may hold values from -0.1875 to 0.1875
- ssm_input: bfloat16 [1024, 1536], P('dp', 'tensor'), may hold values from -0.1875 to 0.1875
- step_weight: bfloat16 [1024, 24], P('dp', 'tensor'), may hold values from -0.09375 to 0.09375
- state_weight: bfloat16 [1024, 256], P('dp'), may hold values from -0.1875 to 0.1875
- conv_input: float32 [4, 1536], P(None, 'tensor'), may hold values from -3 to 3
- input_bias: float32 [1536], P('tensor'), may hold values from -3 to 3
- conv_state: float32 [4, 256], replicated, may hold values from -3 to 3
- state_bias: float32 [256], replicated, may hold values from -3 to 3
- step_bias: float32 [24], P('tensor'), may hold values from -5 to -1
- decay_log: float32 [24], P('tensor'), may hold values from 0 to 2.77
- skip_gain: float32 [24], P('tensor'), may hold values from 0.5 to 1.5
- ssm_norm: float32 [1536], P('tensor'), may hold values from 0.5 to 1.5
- ssm_output: bfloat16 [1536, 1024], P('tensor', 'dp'), may hold values from -0.15625 to 0.15625
- query_weight: bfloat16 [1024, 512], P('dp', 'tensor'), may hold values from -0.1875 to 0.1875
- key_matrix: bfloat16 [1024, 128], P('dp', 'tensor'), may hold values from -0.1875 to 0.1875
- value_matrix: bfloat16 [1024, 128], P('dp', 'tensor'), may hold values from -0.1875 to 0.1875
- output_weight: bfloat16 [512, 1024], P('tensor', 'dp'), may hold values from -2 to 2
- feed_gain: float32 [1024], replicated, may hold values from 0.5 to 1.5
- gate_weight: bfloat16 [1024, 2048], P('dp', 'tensor'), may hold values from -0.1875 to 0.1875
- up_weight: bfloat16 [1024, 2048], P('dp', 'tensor'), may hold values from -0.1875 to 0.1875
- down_weight: bfloat16 [2048, 1024], P('tensor', 'dp'), may hold values from -0.125 to 0.125
- upstream: bfloat16 [16384, 1024], P('dp'), may hold values from -6 to 6
Outputs:
- output: bfloat16 [16384, 1024], P('dp')
- grad_inputs: bfloat16 [16384, 1024], P('dp')
- grad_mixer_gain: float32 [1024], replicated
- grad_ssm_gate: float32 [1024, 1536], P('dp', 'tensor')
- grad_ssm_input: float32 [1024, 1536], P('dp', 'tensor')
- grad_step_weight: float32 [1024, 24], P('dp', 'tensor')
- grad_state_weight: float32 [1024, 256], P('dp')
- grad_conv_input: float32 [4, 1536], P(None, 'tensor')
- grad_input_bias: float32 [1536], P('tensor')
- grad_conv_state: float32 [4, 256], replicated
- grad_state_bias: float32 [256], replicated
- grad_step_bias: float32 [24], P('tensor')
- grad_decay_log: float32 [24], P('tensor')
- grad_skip_gain: float32 [24], P('tensor')
- grad_ssm_norm: float32 [1536], P('tensor')
- grad_ssm_output: float32 [1536, 1024], P('tensor', 'dp')
- grad_query_weight: float32 [1024, 512], P('dp', 'tensor')
- grad_key_weight: float32 [1024, 128], P('dp', 'tensor')
- grad_value_weight: float32 [1024, 128], P('dp', 'tensor')
- grad_output_weight: float32 [512, 1024], P('tensor', 'dp')
- grad_feed_gain: float32 [1024], replicated
- grad_gate_weight: float32 [1024, 2048], P('dp', 'tensor')
- grad_up_weight: float32 [1024, 2048], P('dp', 'tensor')
- grad_down_weight: float32 [2048, 1024], P('tensor', 'dp')
The draws below stay inside these ranges and needn't reach their ends.
Inputs may be any that keep to these rules, and one draw needn't show every extreme that they name: `segments`: in each row the ids never fall, every id from 0 to 3 appears, each covers 1 to 512 positions and one covers exactly 512.
All inputs are finite; a program needn't handle non-finite values.
Results may differ from the reference program's by a relative error of at most 0.018.
Values may be sent and summed in bfloat16 or wider, within the bound.
A program may use at most 192 MiB of HBM per device.

```python
import math
import jax
import jax.numpy as jnp
import numpy as np
from jax import lax

MODEL_WIDTH = 1024
HM = 24
HEAD_SIZE = 64
NS = 128
KC = 4
QUERY_HEADS = 8
KEY_VALUE_HEADS = 2
FF = 2048
LEN = 1024
DOCS = 4
DI = 1536
SEQS = 16
TOKENS = 16384


def steps_of(stream_key, shape, pieces, low, largest):
    level, own = 1.0, jax.random.fold_in(stream_key, 6)
    for dim, parts in pieces:
        steps = jnp.exp(jax.random.uniform(jax.random.fold_in(own, dim), (parts,), jnp.float32, low / len(pieces), largest / len(pieces)))
        level = level * jnp.repeat(steps, shape[dim] // parts).reshape([-1 if axis == dim else 1 for axis in range(len(shape))])
    return level


def profile(count, total, reach, lean):
    portions = [(1 << 20) // math.isqrt(grade ** lean) + 1 for grade in range(2, count + 1)]
    rest, holding = total - reach - (count - 1), [1] * (count - 1)
    while rest > 0:
        candidates = [i for i in range(count - 1) if holding[i] < reach]
        whole, budget = sum([portions[i] for i in candidates]), rest
        for i in candidates:
            extra = min(reach - holding[i], max(1, budget * portions[i] // whole), rest)
            holding[i] = holding[i] + extra
            rest = rest - extra
    return np.array([reach] + holding)


def ragged(rng, number_of, total, reach, skew):
    if number_of == 2:
        one = jax.random.randint(rng, (), max(1, total - reach), min(reach, total - 1) + 1)
        return jnp.stack([one, total - one])
    tallies = jnp.asarray(profile(number_of, total, reach, skew), jnp.int32)
    couples = (number_of - 1) // 2
    source_of, sink = tallies[1:1 + 2 * couples:2], tallies[2:2 + 2 * couples:2]
    margin = jnp.minimum(source_of - 1, reach - sink)
    shifted = jax.random.randint(jax.random.fold_in(rng, 1), (couples,), 0, 1 << 20) % (margin + 1)
    tallies = tallies.at[1:1 + 2 * couples:2].set(source_of - shifted).at[2:2 + 2 * couples:2].set(sink + shifted)
    return tallies[jax.random.permutation(jax.random.fold_in(rng, 2), number_of)]


def gaussian(rng, dims, width, reach, shards=(), kind=jnp.bfloat16):
    values = jax.random.normal(rng, dims, jnp.float32) * width
    if len(shards) > 0:
        values = steps_of(rng, dims, shards, -0.22, 0.18) * values
    return jnp.clip(values, min=-reach, max=reach).astype(kind)


def setup_inputs(seed: int = 0) -> dict:
    key_list = jax.random.split(jax.random.key(seed), 26)
    return {
        "inputs": gaussian(key_list[0], (TOKENS, MODEL_WIDTH), 1.0, 6.0, ((0, 16),)),
        "segments": jax.vmap(lambda own: jnp.searchsorted(jnp.cumsum(ragged(own, DOCS, LEN, LEN // 2, 1)), jnp.arange(LEN), side="right"))(jax.random.split(key_list[1], SEQS)).reshape((SEQS, LEN)).astype(jnp.int32),
        "mixer_gain": jnp.clip(1.0 + 0.1 * jax.random.normal(key_list[2], (MODEL_WIDTH,), jnp.float32), 0.5, 1.5),
        "ssm_gate": gaussian(key_list[3], (MODEL_WIDTH, DI), MODEL_WIDTH ** -0.5, 0.1875, ((0, 16), (1, 2))),
        "ssm_input": gaussian(key_list[4], (MODEL_WIDTH, DI), MODEL_WIDTH ** -0.5, 0.1875, ((0, 16), (1, 2))),
        "step_weight": gaussian(key_list[5], (MODEL_WIDTH, HM), (4 * MODEL_WIDTH) ** -0.5, 0.09375, ((0, 16), (1, 2))),
        "state_weight": gaussian(key_list[6], (MODEL_WIDTH, 2 * NS), MODEL_WIDTH ** -0.5, 0.1875, ((0, 16),)),
        "conv_input": gaussian(key_list[7], (KC, DI), KC ** -0.5, 3.0, ((1, 2),), jnp.float32),
        "input_bias": gaussian(key_list[8], (DI,), 0.5, 3.0, ((0, 2),), jnp.float32),
        "conv_state": gaussian(key_list[9], (KC, 2 * NS), KC ** -0.5, 3.0, (), jnp.float32),
        "state_bias": gaussian(key_list[10], (2 * NS,), 0.5, 3.0, (), jnp.float32),
        "step_bias": jnp.clip(-5.0 + 4.0 * jax.random.uniform(key_list[11], (HM,), jnp.float32) ** steps_of(key_list[11], (HM,), ((0, 2),), -0.2, 0.2), -5.0, -1.0),
        "decay_log": jnp.clip(2.77 * jax.random.uniform(key_list[12], (HM,), jnp.float32) ** steps_of(key_list[12], (HM,), ((0, 2),), -0.2, 0.2), 0.0, 2.77),
        "skip_gain": jnp.clip(0.5 + 1.0 * jax.random.uniform(key_list[13], (HM,), jnp.float32) ** steps_of(key_list[13], (HM,), ((0, 2),), -0.2, 0.2), 0.5, 1.5),
        "ssm_norm": jnp.clip(1.0 + 0.1 * jax.random.normal(key_list[14], (DI,), jnp.float32), 0.5, 1.5),
        "ssm_output": gaussian(key_list[15], (DI, MODEL_WIDTH), DI ** -0.5, 0.15625, ((0, 2), (1, 16))),
        "query_weight": gaussian(key_list[16], (MODEL_WIDTH, QUERY_HEADS * HEAD_SIZE), MODEL_WIDTH ** -0.5, 0.1875, ((0, 16), (1, 2))),
        "key_matrix": gaussian(key_list[17], (MODEL_WIDTH, KEY_VALUE_HEADS * HEAD_SIZE), MODEL_WIDTH ** -0.5, 0.1875, ((0, 16), (1, 2))),
        "value_matrix": gaussian(key_list[18], (MODEL_WIDTH, KEY_VALUE_HEADS * HEAD_SIZE), MODEL_WIDTH ** -0.5, 0.1875, ((0, 16), (1, 2))),
        "output_weight": gaussian(key_list[19], (QUERY_HEADS * HEAD_SIZE, MODEL_WIDTH), (QUERY_HEADS * HEAD_SIZE // 64) ** -0.5, 2.0, ((0, 2), (1, 16))),
        "feed_gain": jnp.clip(1.0 + 0.1 * jax.random.normal(key_list[20], (MODEL_WIDTH,), jnp.float32), 0.5, 1.5),
        "gate_weight": gaussian(key_list[21], (MODEL_WIDTH, FF), MODEL_WIDTH ** -0.5, 0.1875, ((0, 16), (1, 2))),
        "up_weight": gaussian(key_list[22], (MODEL_WIDTH, FF), MODEL_WIDTH ** -0.5, 0.1875, ((0, 16), (1, 2))),
        "down_weight": gaussian(key_list[23], (FF, MODEL_WIDTH), FF ** -0.5, 0.125, ((0, 2), (1, 16))),
        "upstream": gaussian(key_list[24], (TOKENS, MODEL_WIDTH), 1.0, 6.0, ((0, 16),)),
    }


epsilon = 1e-05
rope_base = 100000000000.0
masked_score = -1e+30
highest_precision = lax.Precision.HIGHEST

@jax.custom_vjp
def lowered_forward(v):
    return lax.optimization_barrier(v.astype(jnp.bfloat16)).astype(jnp.float32)

@jax.custom_vjp
def lowered_backward(v):
    return v

def low_keep(v):
    return (lowered_forward(v), None)

def low_pass(kept, grad):
    return (grad,)

def back_keep(v):
    return (v, None)

def back_low(kept, grad):
    return (lowered_forward(grad),)
lowered_forward.defvjp(low_keep, low_pass)
lowered_backward.defvjp(back_keep, back_low)

def matrix_product(left, right):
    return jnp.dot(left, right, precision=highest_precision, preferred_element_type=jnp.float32)

def rms_scale(values):
    return lax.rsqrt(lax.optimization_barrier(jnp.mean(values * values, axis=-1, keepdims=True)) + epsilon)

def causal_conv(segment_ids, values, weights, biases):
    tap_count = weights.shape[0]
    summed = biases[None, :] + weights[tap_count - 1][None, :] * values
    for offset in range(1, tap_count):
        earlier = jnp.pad(values, ((offset, 0), (0, 0)))[:-offset]
        earlier_ids = jnp.pad(segment_ids, (offset, 0), constant_values=-1)[:-offset]
        summed = summed + weights[tap_count - 1 - offset][None, :] * jnp.where((earlier_ids == segment_ids)[:, None], earlier, 0.0)
    return jax.nn.silu(summed)

def rope_tables(sequence_length, head_width):
    half_width = head_width // 2
    frequency = rope_base ** (-2.0 * jnp.arange(half_width, dtype=jnp.float32) / head_width)
    angles = jnp.arange(sequence_length, dtype=jnp.float32)[:, None] * frequency[None, :]
    return (jnp.cos(angles), jnp.sin(angles))

def apply_rotation(vectors, cosine_table, sine_table):
    half_width = vectors.shape[-1] // 2
    shape_out = (vectors.shape[0],) + (1,) * (vectors.ndim - 2) + (half_width,)
    cos_part = cosine_table.reshape(shape_out)
    sin_part = sine_table.reshape(shape_out)
    first_half = vectors[..., :half_width]
    second_half = vectors[..., half_width:]
    return jnp.concatenate([first_half * cos_part - second_half * sin_part, second_half * cos_part + first_half * sin_part], axis=-1)

def state_mix(heads_in, step_size, rate, state_in, state_out, segment_ids):
    sequence_length = heads_in.shape[0]
    cumulative = jnp.cumsum(-step_size * rate[None, :], axis=0).T
    positions = jnp.arange(sequence_length)
    allowed = (positions[:, None] >= positions[None, :]) & (segment_ids[:, None] == segment_ids[None, :])
    spread = cumulative[:, :, None] - cumulative[:, None, :]
    decays = jnp.where(allowed[None], jnp.exp(jnp.where(allowed[None], spread, 0.0)), 0.0)
    intersection = matrix_product(state_out, state_in.T)
    scaled_in = heads_in * step_size[:, :, None]
    return jnp.einsum('hts,shp->thp', decays * intersection[None], scaled_in, precision=highest_precision)

def block(inputs, segment_ids, params):
    mixer_gain, ssm_gate, ssm_input, step_weight, state_weight, conv_input, input_bias, conv_state, state_bias, step_bias, decay_log, skip_gain, ssm_norm, ssm_output, query_weight, key_matrix, value_matrix, output_weight, feed_gain, gate_weight, up_weight, down_weight = params
    sequence_length = inputs.shape[0]
    hidden_activations = lowered_forward(inputs * rms_scale(inputs) * mixer_gain)
    gate_z = lowered_backward(matrix_product(hidden_activations, ssm_gate))
    inner_raw = lowered_backward(matrix_product(hidden_activations, ssm_input))
    step_raw = lowered_backward(matrix_product(hidden_activations, step_weight))
    state_raw = lowered_backward(matrix_product(hidden_activations, state_weight))
    inner_conv = causal_conv(segment_ids, inner_raw, conv_input, input_bias)
    state_conv = causal_conv(segment_ids, state_raw, conv_state, state_bias)
    step_size = jax.nn.softplus(step_raw + step_bias)
    heads_in = inner_conv.reshape(sequence_length, HM, HEAD_SIZE)
    ssm_mixed = state_mix(heads_in, step_size, jnp.exp(decay_log), state_conv[:, :NS], state_conv[:, NS:], segment_ids)
    ssm_mixed = ssm_mixed + skip_gain[None, :, None] * heads_in
    gated_ssm = ssm_mixed.reshape(sequence_length, HM * HEAD_SIZE) * jax.nn.silu(gate_z)
    normed = lowered_forward(gated_ssm * rms_scale(gated_ssm) * ssm_norm)
    ssm_out = lowered_backward(matrix_product(normed, ssm_output))
    cosine_table, sine_table = rope_tables(sequence_length, HEAD_SIZE)
    query_rows = apply_rotation(lowered_backward(matrix_product(hidden_activations, query_weight)).reshape(sequence_length, QUERY_HEADS, HEAD_SIZE), cosine_table, sine_table)
    projected_keys = apply_rotation(lowered_backward(matrix_product(hidden_activations, key_matrix)).reshape(sequence_length, KEY_VALUE_HEADS, HEAD_SIZE), cosine_table, sine_table)
    projected_values = lowered_forward(lowered_backward(matrix_product(hidden_activations, value_matrix))).reshape(sequence_length, KEY_VALUE_HEADS, HEAD_SIZE)
    query_rows = lowered_forward(query_rows).reshape(sequence_length, KEY_VALUE_HEADS, QUERY_HEADS // KEY_VALUE_HEADS, HEAD_SIZE)
    projected_keys = lowered_forward(projected_keys)
    attention_scores = lowered_backward(jnp.einsum('havb,oab->avho', query_rows, projected_keys, precision=highest_precision) / math.sqrt(HEAD_SIZE))
    positions = jnp.arange(sequence_length)
    allowed = (positions[:, None] >= positions[None, :]) & (segment_ids[:, None] == segment_ids[None, :])
    attention_scores = jnp.where(allowed, attention_scores, masked_score)
    attention_weights = jax.nn.softmax(attention_scores, axis=-1)
    attention_result = lowered_backward(jnp.einsum('woyu,uwq->ywoq', lowered_forward(attention_weights), projected_values, precision=highest_precision))
    attn_out = lowered_backward(matrix_product(lowered_forward(attention_result.reshape(sequence_length, QUERY_HEADS * HEAD_SIZE)), output_weight))
    middle = inputs + ssm_out + attn_out
    hidden_two = lowered_forward(middle * rms_scale(middle) * feed_gain)
    gate_value = lowered_backward(matrix_product(hidden_two, gate_weight))
    up_value = lowered_backward(matrix_product(hidden_two, up_weight))
    product = lowered_forward(jax.nn.silu(gate_value) * up_value)
    return middle + lowered_backward(matrix_product(product, down_weight))

def reference(inputs, segments, mixer_gain, ssm_gate, ssm_input, step_weight, state_weight, conv_input, input_bias, conv_state, state_bias, step_bias, decay_log, skip_gain, ssm_norm, ssm_output, query_weight, key_matrix, value_matrix, output_weight, feed_gain, gate_weight, up_weight, down_weight, upstream):
    params = tuple((weight.astype(jnp.float32) for weight in (mixer_gain, ssm_gate, ssm_input, step_weight, state_weight, conv_input, input_bias, conv_state, state_bias, step_bias, decay_log, skip_gain, ssm_norm, ssm_output, query_weight, key_matrix, value_matrix, output_weight, feed_gain, gate_weight, up_weight, down_weight)))

    def whole(flat_inputs, weight_set):
        sequences = flat_inputs.reshape(segments.shape[0], segments.shape[1], flat_inputs.shape[1])

        def one_sequence(packed):
            return block(packed[0], packed[1], weight_set)
        results = lax.map(jax.checkpoint(one_sequence), (sequences, segments))
        return results.reshape(flat_inputs.shape)
    result, pullback = jax.vjp(whole, inputs.astype(jnp.float32), params)
    grad_inputs, grads = pullback(upstream.astype(jnp.float32))
    return (result.astype(jnp.bfloat16), grad_inputs.astype(jnp.bfloat16), grads[0], grads[1], grads[2], grads[3], grads[4], grads[5], grads[6], grads[7], grads[8], grads[9], grads[10], grads[11], grads[12], grads[13], grads[14], grads[15], grads[16], grads[17], grads[18], grads[19], grads[20], grads[21])
```

```python
from functools import partial
import math

import jax
import jax.numpy as jnp
from jax import lax
from jax.sharding import PartitionSpec as P

HM = 24
HEAD_SIZE = 64
BLK = 128


epsilon = 1e-05
rope_base = 100000000000.0
masked_score = -1e30
mix_precision = lax.Precision.HIGH
STEP_PAD = 128


def swap_tensor(values):
    return lax.ppermute(values, "tensor", [(0, 1), (1, 0)])


def pair_sum(values):
    low = lax.reduce_precision(values, 8, 7)
    return low + swap_tensor(low.astype(jnp.bfloat16)).astype(jnp.float32)


def pair_sum_wide(values):
    return values + swap_tensor(values)


def bit_orders(count):
    bits = list(range(count.bit_length() - 1))
    return bits, bits[1::-1] + bits[2:]


def partners(count, bit):
    return [(i, i ^ (1 << bit)) for i in range(count)]


def gather_rows(shard, order):
    count = lax.axis_size("dp")
    place = lax.axis_index("dp")
    held = shard
    done = []
    for bit in reversed(order):
        other = lax.ppermute(held, "dp", partners(count, bit))
        low_side = (place >> bit) & 1 == 0
        axis = sum(earlier > bit for earlier in done)
        held = jnp.stack(
            [jnp.where(low_side, held, other), jnp.where(low_side, other, held)], axis=axis
        )
        done.append(bit)
    return held.reshape(count * shard.shape[0], shard.shape[1])


def scatter_rows(partial_sum, order):
    count = lax.axis_size("dp")
    place = lax.axis_index("dp")
    rows = partial_sum.shape[0] // count
    left = sorted(order, reverse=True)
    held = partial_sum.reshape((2,) * len(left) + (rows, partial_sum.shape[1]))
    for bit in order:
        axis = left.index(bit)
        side = (place >> bit) & 1
        mine = lax.dynamic_index_in_dim(held, side, axis, keepdims=False)
        theirs = lax.dynamic_index_in_dim(held, 1 - side, axis, keepdims=False)
        came = lax.ppermute(theirs.astype(jnp.bfloat16), "dp", partners(count, bit))
        held = mine + came.astype(jnp.float32)
        left.remove(bit)
    return held


def sum_all(vector):
    count = lax.axis_size("dp")
    for bit in range(count.bit_length() - 1):
        vector = vector + lax.ppermute(vector, "dp", partners(count, bit))
    return vector


def forward_dot(left, right):
    return jnp.dot(left, right, preferred_element_type=jnp.float32)


def back_dot(grad_rows, weights):
    return jnp.einsum("tj,ij->ti", grad_rows, weights, preferred_element_type=jnp.float32)


def outer_sum(left, right):
    return jnp.einsum("ti,tj->ij", left, right, preferred_element_type=jnp.float32)


def rms_scale(values):
    return lax.rsqrt(jnp.mean(values * values, axis=-1, keepdims=True) + epsilon)


def norm_back(values, score_scale, gain, grad_normed):
    scaled_grad = grad_normed * gain
    grad_values = score_scale * scaled_grad - values * score_scale**3 * jnp.mean(
        scaled_grad * values, axis=-1, keepdims=True
    )
    grad_gain = jnp.sum(grad_normed * values * score_scale, axis=0)
    return (grad_values, grad_gain)


def causal_conv(segment_ids, values, weights, biases):
    tap_count = weights.shape[0]
    summed = biases[None, :] + weights[tap_count - 1][None, :] * values
    for offset in range(1, tap_count):
        earlier = jnp.pad(values, ((offset, 0), (0, 0)))[:-offset]
        earlier_ids = jnp.pad(segment_ids, (offset, 0), constant_values=-1)[:-offset]
        summed = summed + weights[tap_count - 1 - offset][None, :] * jnp.where(
            (earlier_ids == segment_ids)[:, None], earlier, 0.0
        )
    return jax.nn.silu(summed)


def rope_tables(sequence_length, head_width):
    half_width = head_width // 2
    frequency = rope_base ** (-2.0 * jnp.arange(half_width, dtype=jnp.float32) / head_width)
    angles = jnp.arange(sequence_length, dtype=jnp.float32)[:, None] * frequency[None, :]
    return (jnp.cos(angles), jnp.sin(angles))


def turn(vectors, cosine_table, sine_table, direction):
    half_width = vectors.shape[-1] // 2
    shape_out = (vectors.shape[0],) + (1,) * (vectors.ndim - 2) + (half_width,)
    cos_part = cosine_table.reshape(shape_out)
    sin_part = direction * sine_table.reshape(shape_out)
    first_half = vectors[..., :half_width]
    second_half = vectors[..., half_width:]
    return jnp.concatenate(
        [
            first_half * cos_part - second_half * sin_part,
            second_half * cos_part + first_half * sin_part,
        ],
        axis=-1,
    )


def span_mix(heads_in, step_size, rate, state_in, state_out, segment_ids):
    sequence_length, head_count, head_width = heads_in.shape
    block_count = sequence_length // BLK
    states = state_in.shape[1]
    offsets = jnp.arange(BLK)
    lower = (offsets[:, None] >= offsets[None, :]).astype(jnp.float32)
    cumulative = jnp.einsum(
        "ts,nsh->nht",
        lower,
        (-step_size * rate[None, :]).reshape(block_count, BLK, head_count),
        precision=lax.Precision.HIGHEST,
    )
    block_ids = segment_ids.reshape(block_count, BLK)
    scaled_in = (heads_in * step_size[:, :, None]).reshape(block_count, BLK, head_count, head_width)
    in_blocks = state_in.reshape(block_count, BLK, states)
    out_blocks = state_out.reshape(block_count, BLK, states)
    allowed = (offsets[:, None] >= offsets[None, :])[None] & (
        block_ids[:, :, None] == block_ids[:, None, :]
    )
    spread = cumulative[:, :, :, None] - cumulative[:, :, None, :]
    decays = jnp.where(allowed[:, None], jnp.exp(jnp.where(allowed[:, None], spread, 0.0)), 0.0)
    intersection = jnp.einsum("ntk,nsk->nts", out_blocks, in_blocks, precision=mix_precision)
    inside = jnp.einsum(
        "nhts,nshp->nthp", decays * intersection[:, None], scaled_in, precision=mix_precision
    )
    last_ids = block_ids[:, -1]
    to_end = jnp.where(
        (block_ids == last_ids[:, None])[:, None, :],
        jnp.exp(cumulative[:, :, -1:] - cumulative),
        0.0,
    )
    local_state = jnp.einsum(
        "nhs,nshp,nsk->nhpk", to_end, scaled_in, in_blocks, precision=mix_precision
    )
    carried = jnp.concatenate([jnp.zeros((1,), dtype=bool), last_ids[1:] == last_ids[:-1]])

    factors = jnp.where(carried[:, None], jnp.exp(cumulative[:, :, -1]), 0.0)
    running = jnp.zeros(local_state.shape[1:], local_state.dtype)
    entering = [running]
    for block in range(block_count - 1):
        running = factors[block][:, None, None] * running + local_state[block]
        entering.append(running)
    entering = jnp.stack(entering)
    earlier_ids = jnp.concatenate([jnp.full((1,), -1, jnp.int32), last_ids[:-1]])
    from_start = jnp.where(
        (block_ids == earlier_ids[:, None])[:, None, :], jnp.exp(cumulative), 0.0
    )
    across = (
        jnp.einsum("ntk,nhpk->nthp", out_blocks, entering, precision=mix_precision)
        * from_start.transpose(0, 2, 1)[:, :, :, None]
    )
    return (inside + across).reshape(sequence_length, head_count, head_width)


def ssm_core(
    segment_ids,
    inner_raw,
    state_conv,
    step_raw,
    gate_z,
    conv_input,
    input_bias,
    step_bias,
    decay_log,
    skip_gain,
):
    sequence_length = inner_raw.shape[0]
    head_count = step_raw.shape[1]
    inner_conv = causal_conv(segment_ids, inner_raw, conv_input, input_bias)
    step_size = jax.nn.softplus(step_raw + step_bias)
    heads_in = inner_conv.reshape(sequence_length, head_count, -1)
    states = state_conv.shape[1] // 2
    ssm_mixed = span_mix(
        heads_in,
        step_size,
        jnp.exp(decay_log),
        state_conv[:, :states],
        state_conv[:, states:],
        segment_ids,
    )
    ssm_mixed = ssm_mixed + skip_gain[None, :, None] * heads_in
    return ssm_mixed.reshape(sequence_length, -1) * jax.nn.silu(gate_z)


def block_scores(query_rows, projected_keys, segment_ids, first_row, score_scale):
    row_count = query_rows.shape[0]
    raw_scores = (
        jnp.einsum("havb,oab->avho", query_rows, projected_keys, preferred_element_type=jnp.float32)
        * score_scale
    )
    query_pos = first_row + jnp.arange(row_count)
    key_pos = jnp.arange(segment_ids.shape[0])
    query_ids = lax.dynamic_slice_in_dim(segment_ids, first_row, row_count)
    allowed = (query_pos[:, None] >= key_pos[None, :]) & (
        query_ids[:, None] == segment_ids[None, :]
    )
    return jnp.where(allowed, raw_scores, masked_score)


def on_device(
    inputs,
    segments,
    mixer_gain,
    ssm_gate,
    ssm_input,
    step_weight,
    state_weight,
    conv_input,
    input_bias,
    conv_state,
    state_bias,
    step_bias,
    decay_log,
    skip_gain,
    ssm_norm,
    ssm_output,
    query_weight,
    key_matrix,
    value_matrix,
    output_weight,
    feed_gain,
    gate_weight,
    up_weight,
    down_weight,
    upstream,
):
    segment_ids = segments.reshape(-1)
    sequence_length = inputs.shape[0]
    order_a, order_b = bit_orders(lax.axis_size("dp"))
    inner_width = ssm_input.shape[1]
    step_width = step_weight.shape[1]
    query_width = query_weight.shape[1]
    key_width = key_matrix.shape[1]
    main_width = inner_width + STEP_PAD
    step_padding = ((0, 0), (0, STEP_PAD - step_width))
    side_a = gather_rows(
        jnp.concatenate([ssm_input, jnp.pad(step_weight, step_padding), state_weight], axis=1),
        order_a,
    )
    side_b = gather_rows(
        jnp.concatenate([ssm_gate, query_weight, key_matrix, value_matrix], axis=1), order_b
    )
    mixer_out_local = jnp.concatenate([ssm_output, output_weight], axis=0).T
    mixer_out_local, gate_local, up_local, down_local, side_a, side_b = lax.optimization_barrier(
        (mixer_out_local, gate_weight, up_weight, down_weight.T, side_a, side_b)
    )
    mixer_out = gather_rows(mixer_out_local, order_a)
    full_down = gather_rows(down_local, order_b)
    full_feed_gate = gather_rows(gate_local, order_a)
    full_feed_up = gather_rows(up_local, order_b)
    tokens = inputs.astype(jnp.float32)
    first_scale = rms_scale(tokens)
    hidden_activations = (tokens * first_scale * mixer_gain).astype(jnp.bfloat16)
    raw_a = forward_dot(hidden_activations, side_a)
    raw_b = forward_dot(hidden_activations, side_b)
    inner_raw = raw_a[:, :inner_width]
    step_raw = raw_a[:, inner_width : inner_width + step_width]
    state_raw = raw_a[:, main_width:]
    gate_z = raw_b[:, :inner_width]
    query_raw, key_raw, value_raw = jnp.split(
        raw_b[:, inner_width:], [query_width, query_width + key_width], axis=1
    )
    state_conv, state_pull = jax.vjp(
        partial(causal_conv, segment_ids), state_raw, conv_state, state_bias
    )
    gated_ssm, ssm_pull = jax.vjp(
        partial(ssm_core, segment_ids),
        inner_raw,
        state_conv,
        step_raw,
        gate_z,
        conv_input,
        input_bias,
        step_bias,
        decay_log,
        skip_gain,
    )
    all_squares = pair_sum_wide(jnp.sum(gated_ssm * gated_ssm, axis=-1, keepdims=True))
    ssm_scale = lax.rsqrt(all_squares / (HM * HEAD_SIZE) + epsilon)
    normed = (gated_ssm * ssm_scale * ssm_norm).astype(jnp.bfloat16)
    local_kv = key_raw.shape[1] // HEAD_SIZE
    group_size = query_raw.shape[1] // HEAD_SIZE // local_kv
    score_scale = 1.0 / math.sqrt(HEAD_SIZE)
    cosine_table, sine_table = rope_tables(sequence_length, HEAD_SIZE)
    query_rows = turn(
        query_raw.reshape(sequence_length, local_kv, group_size, HEAD_SIZE),
        cosine_table,
        sine_table,
        1.0,
    ).astype(jnp.bfloat16)
    projected_keys = turn(
        key_raw.reshape(sequence_length, local_kv, HEAD_SIZE), cosine_table, sine_table, 1.0
    ).astype(jnp.bfloat16)
    projected_values = value_raw.reshape(sequence_length, local_kv, HEAD_SIZE).astype(jnp.bfloat16)
    block_rows = min(512, sequence_length)
    attended_parts = []
    log_totals = []
    for first_row in range(0, sequence_length, block_rows):
        attention_scores = block_scores(
            query_rows[first_row : first_row + block_rows],
            projected_keys,
            segment_ids,
            first_row,
            score_scale,
        )
        row_max = jnp.max(attention_scores, axis=-1, keepdims=True)
        exponent = jnp.exp(attention_scores - row_max)
        row_total = jnp.sum(exponent, axis=-1, keepdims=True)
        attention_lowered = (exponent / row_total).astype(jnp.bfloat16)
        attended_parts.append(
            jnp.einsum(
                "woyu,uwq->ywoq",
                attention_lowered,
                projected_values,
                preferred_element_type=jnp.float32,
            )
        )
        log_totals.append(row_max + jnp.log(row_total))
    attention_result = (
        jnp.concatenate(attended_parts, axis=0).reshape(sequence_length, -1).astype(jnp.bfloat16)
    )
    mixer_in = jnp.concatenate([normed, attention_result], axis=1)
    middle = tokens + pair_sum(back_dot(mixer_in, mixer_out))
    second_scale = rms_scale(middle)
    hidden_two = (middle * second_scale * feed_gain).astype(jnp.bfloat16)
    gate_value = forward_dot(hidden_two, full_feed_gate)
    up_value = forward_dot(hidden_two, full_feed_up)
    product = (jax.nn.silu(gate_value) * up_value).astype(jnp.bfloat16)
    feed_out = pair_sum(back_dot(product, full_down))
    output = (middle + feed_out).astype(jnp.bfloat16)
    down_shard = scatter_rows(outer_sum(upstream, product), order_b).T
    grad_product = forward_dot(upstream, full_down)
    gate_sigmoid = jax.nn.sigmoid(gate_value)
    grad_gate = (
        grad_product * up_value * gate_sigmoid * (1.0 + gate_value * (1.0 - gate_sigmoid))
    ).astype(jnp.bfloat16)
    grad_up = (grad_product * jax.nn.silu(gate_value)).astype(jnp.bfloat16)
    feed_gate_shard = scatter_rows(outer_sum(hidden_two, grad_gate), order_a)
    feed_up_shard = scatter_rows(outer_sum(hidden_two, grad_up), order_b)
    grad_hidden_two = pair_sum(
        back_dot(grad_gate, full_feed_gate) + back_dot(grad_up, full_feed_up)
    )
    grad_mid_norm, grad_feed_gain = norm_back(middle, second_scale, feed_gain, grad_hidden_two)
    grad_middle = upstream.astype(jnp.float32) + grad_mid_norm
    grad_branch = grad_middle.astype(jnp.bfloat16)
    mixer_out_shard = scatter_rows(outer_sum(grad_branch, mixer_in), order_a).T
    grad_mixer_in = forward_dot(grad_branch, mixer_out)
    grad_normed = grad_mixer_in[:, :inner_width]
    grad_attended = (
        grad_mixer_in[:, inner_width:]
        .astype(jnp.bfloat16)
        .reshape(sequence_length, local_kv, group_size, HEAD_SIZE)
    )
    scaled_grad = grad_normed * ssm_norm
    grad_ssm_norm = jnp.sum(grad_normed * gated_ssm * ssm_scale, axis=0)
    cross_sum = pair_sum_wide(jnp.sum(scaled_grad * gated_ssm, axis=-1, keepdims=True))
    grad_gated = ssm_scale * scaled_grad - gated_ssm * ssm_scale**3 * cross_sum / (HM * HEAD_SIZE)
    (
        grad_inner,
        grad_state_conv,
        grad_step_raw,
        grad_gate_z,
        grad_conv_input,
        grad_input_bias,
        grad_step_bias,
        grad_decay_log,
        grad_skip_gain,
    ) = ssm_pull(grad_gated)
    grad_query_parts = []
    grad_key_sum = jnp.zeros((sequence_length, local_kv, HEAD_SIZE), jnp.float32)
    grad_value_sum = jnp.zeros((sequence_length, local_kv, HEAD_SIZE), jnp.float32)
    for block_index, first_row in enumerate(range(0, sequence_length, block_rows)):
        query_tile_rows = query_rows[first_row : first_row + block_rows]
        block_gradient = grad_attended[first_row : first_row + block_rows]
        attention_scores = block_scores(
            query_tile_rows, projected_keys, segment_ids, first_row, score_scale
        )
        attention_weights = jnp.exp(attention_scores - log_totals[block_index])
        grad_probs = jnp.einsum(
            "havb,oab->avho", block_gradient, projected_values, preferred_element_type=jnp.float32
        )
        inner_term = jnp.sum(grad_probs * attention_weights, axis=-1, keepdims=True)
        score_gradient = (attention_weights * (grad_probs - inner_term)).astype(jnp.bfloat16)
        grad_query_parts.append(
            jnp.einsum(
                "woyu,uwq->ywoq", score_gradient, projected_keys, preferred_element_type=jnp.float32
            )
            * score_scale
        )
        grad_key_sum = (
            grad_key_sum
            + jnp.einsum(
                "mhvu,vmhi->umi",
                score_gradient,
                query_tile_rows,
                preferred_element_type=jnp.float32,
            )
            * score_scale
        )
        grad_value_sum = grad_value_sum + jnp.einsum(
            "mhvu,vmhi->umi",
            attention_weights.astype(jnp.bfloat16),
            block_gradient,
            preferred_element_type=jnp.float32,
        )
    grad_query = (
        turn(jnp.concatenate(grad_query_parts, axis=0), cosine_table, sine_table, -1.0)
        .reshape(sequence_length, -1)
        .astype(jnp.bfloat16)
    )
    grad_key = (
        turn(grad_key_sum, cosine_table, sine_table, -1.0)
        .reshape(sequence_length, -1)
        .astype(jnp.bfloat16)
    )
    grad_value = grad_value_sum.reshape(sequence_length, -1).astype(jnp.bfloat16)
    state_sum = pair_sum(grad_state_conv)
    grads_b = jnp.concatenate(
        [grad_gate_z.astype(jnp.bfloat16), grad_query, grad_key, grad_value], axis=1
    )
    shard_b = scatter_rows(outer_sum(hidden_activations, grads_b), order_b)
    grads_main = jnp.concatenate(
        [
            grad_inner.astype(jnp.bfloat16),
            jnp.pad(grad_step_raw.astype(jnp.bfloat16), step_padding),
        ],
        axis=1,
    )
    hidden_sum = pair_sum(back_dot(grads_b, side_b) + back_dot(grads_main, side_a[:, :main_width]))
    grad_state_raw, grad_conv_state, grad_state_bias = state_pull(state_sum)
    grad_state_low = grad_state_raw.astype(jnp.bfloat16)
    shard_a = scatter_rows(
        outer_sum(hidden_activations, jnp.concatenate([grads_main, grad_state_low], axis=1)),
        order_a,
    )
    grad_hidden = hidden_sum + back_dot(grad_state_low, side_a[:, main_width:])
    grad_in_norm, grad_mixer_gain = norm_back(tokens, first_scale, mixer_gain, grad_hidden)
    grad_inputs = (grad_middle + grad_in_norm).astype(jnp.bfloat16)
    small_parts = (
        grad_mixer_gain,
        grad_conv_input,
        grad_input_bias,
        grad_conv_state,
        grad_state_bias,
        grad_ssm_norm,
        grad_feed_gain,
        grad_step_bias,
        grad_decay_log,
        grad_skip_gain,
    )
    packed = jnp.concatenate([part.reshape(-1) for part in small_parts])
    packed = jnp.pad(packed, (0, -packed.shape[0] % 1024)).reshape(-1, 128)
    packed = sum_all(packed).reshape(-1)
    small_sums = []
    first = 0
    for part in small_parts:
        small_sums.append(packed[first : first + part.size].reshape(part.shape))
        first += part.size
    value_first = inner_width + query_width + key_width
    return (
        output,
        grad_inputs,
        small_sums[0],
        shard_b[:, :inner_width],
        shard_a[:, :inner_width],
        shard_a[:, inner_width : inner_width + step_width],
        shard_a[:, main_width:],
        small_sums[1],
        small_sums[2],
        small_sums[3],
        small_sums[4],
        small_sums[7],
        small_sums[8],
        small_sums[9],
        small_sums[5],
        mixer_out_shard[:inner_width],
        shard_b[:, inner_width : inner_width + query_width],
        shard_b[:, inner_width + query_width : value_first],
        shard_b[:, value_first:],
        mixer_out_shard[inner_width:],
        small_sums[6],
        feed_gate_shard,
        feed_up_shard,
        down_shard,
    )


def solution(mesh):
    return jax.shard_map(
        on_device,
        mesh=mesh,
        in_specs=(
            P("dp", None),
            P("dp", None),
            P(),
            P("dp", "tensor"),
            P("dp", "tensor"),
            P("dp", "tensor"),
            P("dp", None),
            P(None, "tensor"),
            P("tensor"),
            P(),
            P(),
            P("tensor"),
            P("tensor"),
            P("tensor"),
            P("tensor"),
            P("tensor", "dp"),
            P("dp", "tensor"),
            P("dp", "tensor"),
            P("dp", "tensor"),
            P("tensor", "dp"),
            P(),
            P("dp", "tensor"),
            P("dp", "tensor"),
            P("tensor", "dp"),
            P("dp", None),
        ),
        out_specs=(
            P("dp", None),
            P("dp", None),
            P(),
            P("dp", "tensor"),
            P("dp", "tensor"),
            P("dp", "tensor"),
            P("dp", None),
            P(None, "tensor"),
            P("tensor"),
            P(),
            P(),
            P("tensor"),
            P("tensor"),
            P("tensor"),
            P("tensor"),
            P("tensor", "dp"),
            P("dp", "tensor"),
            P("dp", "tensor"),
            P("dp", "tensor"),
            P("tensor", "dp"),
            P(),
            P("dp", "tensor"),
            P("dp", "tensor"),
            P("tensor", "dp"),
        ),
        check_vma=False,
    )
```
